128 devices in a mesh: sub: 8 (over x_hi, z), stn: 16 (over y, x_lo, core).
Axes of the slice: x: 4 (x_hi: 2, x_lo: 2; x = x_hi * 2 + x_lo), y: 4, z: 4, core: 2. Of those that a mesh axis runs over, the one named last changes fastest.
Arguments:
- samples: bfloat16 [512, 524288], P('stn', 'sub'), may hold values from -8 to 7, as said below
- taps: int32 [4096], replicated, may hold values from -64 to 64
Outputs:
- visibility: bfloat16 [16, 512, 288, 128], P('sub', 'stn')
The draws below stay inside these ranges and needn't reach their ends.
Inputs may be any that keep to these rules, and one draw needn't show every extreme that they name: `samples`: whole numbers.
All inputs are finite; a program needn't handle non-finite values.
Results may differ from the reference program's by a relative error of at most 0.0073.
Values may be sent and summed in bfloat16 or wider, within the bound.
No kernel may reach another device: no remote copies, remote signals or barrier semaphores. Data moves between devices by JAX's collectives and lax.ppermute only.
A program may use at most 128 MiB of HBM per device.

```python
import math
import jax
import jax.numpy as jnp
from jax import lax

BRANCHES = 256
TAPS = 16
LAGS = 128
SUB_DEV = 2
T_DEV = 256
INPUTS = 512
SAMPLES = 524288
N_SUB = 8
N_STN = 16


def draw_samples(key, part):
    key = jax.random.fold_in(key, 11)
    values = jax.random.randint(key, (INPUTS, SAMPLES), -8, 8)
    return values.astype(jnp.float32).astype(jnp.bfloat16)


def plant(entries, stream_key, least, top_value):
    longest = entries.shape.index(max(entries.shape))
    spots = []
    for shift in (0, 1):
        where = [jax.random.randint(jax.random.fold_in(stream_key, axis), (), 0, length) for axis, length in enumerate(entries.shape)]
        where[longest] = (where[longest] + shift) % entries.shape[longest]
        spots.append(tuple(where))
    return entries.at[spots[0]].set(least).at[spots[1]].set(top_value)


def setup_inputs(seed: int = 0) -> dict:
    streams_of = jax.random.split(jax.random.key(seed), 3)
    samples = draw_samples(jax.random.fold_in(streams_of[2], 71), 0)
    taps = plant(jax.random.randint(streams_of[1], (TAPS * BRANCHES,), -64, 65), jax.random.fold_in(streams_of[1], 1), -64, 64).astype(jnp.int32)
    return dict(samples=samples, taps=taps)


def cosine_matrix(count, branches):
    band = (branches // 2 - count // 2 + jnp.arange(count, dtype=jnp.int32)).astype(jnp.float32) + 0.5
    filter_arm = jnp.arange(branches, dtype=jnp.int32).astype(jnp.float32) + 0.5
    values = jnp.cos(math.pi / branches * band[:, None] * filter_arm[None, :]) * (math.sqrt(2.0 / branches) / 512.0)
    return values.astype(jnp.bfloat16)

def correlate(own, partner, half):
    length = own.shape[-1]
    padded_own = jnp.pad(own, ((0, 0), (half, half)))
    starts = half - jnp.arange(half, dtype=jnp.int32)

    def take(start):
        return lax.dynamic_slice_in_dim(padded_own, start, length + half, axis=1)
    toeplitz_matrix = jax.vmap(take)(starts)
    padded = jnp.pad(partner, ((0, 0), (half, half)))
    lower = jnp.einsum('lau,bu->abl', toeplitz_matrix, padded[:, :length + half])
    upper = jnp.einsum('lau,bu->abl', toeplitz_matrix, padded[:, half:])
    return jnp.concatenate([lower, upper], axis=-1)

def reference(samples, taps):
    inputs = samples.shape[0]
    block = inputs // N_STN
    window = SUB_DEV * N_SUB
    total = T_DEV * N_SUB
    reach = N_STN // 2
    half = LAGS // 2
    scale = 1.0 / math.sqrt(T_DEV * N_SUB)
    table = cosine_matrix(window, BRANCHES).astype(jnp.float32)
    tap_table = taps.reshape(TAPS, BRANCHES).astype(jnp.float32)

    def filter_block(rows):
        extended = jnp.pad(rows.astype(jnp.float32), ((0, 0), ((TAPS - 1) * BRANCHES, 0)))
        frames = extended.reshape(block, total + TAPS - 1, BRANCHES)
        filtered = tap_table[0] * frames[:, 0:total]
        for step in range(1, TAPS):
            filtered = filtered + tap_table[step] * frames[:, step:step + total]
        rounded_values = filtered.astype(jnp.bfloat16).astype(jnp.float32)
        spectra = jnp.einsum('sm,ifm->sif', table, rounded_values, precision=lax.Precision.HIGHEST)
        return spectra.astype(jnp.bfloat16)
    bands = lax.map(filter_block, samples.reshape(N_STN, block, SAMPLES))
    bands = jnp.transpose(bands, (1, 0, 2, 3)).reshape(window, inputs, total)

    def one_band(band):
        rows = band.astype(jnp.float32).reshape(N_STN, block, total)

        def one_block(index):
            own = rows[index]
            partners = jnp.roll(rows, -index, axis=0)[:reach + 1].reshape((reach + 1) * block, total)
            return (correlate(own, partners, half) * scale).astype(jnp.bfloat16)
        result = lax.map(one_block, jnp.arange(N_STN, dtype=jnp.int32))
        return result.reshape(inputs, (reach + 1) * block, LAGS)
    return lax.map(one_band, bands)
```

```python
import functools
import math

import jax
import jax.numpy as jnp
import numpy as np
from jax import lax
from jax.experimental import pallas as pl
from jax.experimental.pallas import tpu as pltpu
from jax.sharding import Mesh
from jax.sharding import PartitionSpec as P

BRANCHES = 256
TAPS = 16
LAGS = 128
T_DEV = 256
SUBBANDS = 16
BLOCK = 32
N_SUB = 8
CHIPS = 8
TOTAL = T_DEV * N_SUB
TAIL = 128
CHUNK = 32
REACH = 4
LANE = 128


def cosine_matrix():
    band = np.float32(BRANCHES // 2 - SUBBANDS // 2) + np.arange(SUBBANDS, dtype=np.float32)
    band = band + np.float32(0.5)
    arm = np.arange(BRANCHES, dtype=np.float32) + np.float32(0.5)
    angle = np.float32(math.pi / BRANCHES) * band[:, None] * arm[None, :]
    table = np.cos(angle) * np.float32(math.sqrt(2.0 / BRANCHES) / 512.0)
    return jnp.asarray(table).astype(jnp.bfloat16).astype(jnp.float32)


def nt_dot(a, b):
    return lax.dot_general(a, b, (((1,), (1,)), ((), ())), preferred_element_type=jnp.float32)


def shift_lanes(tiles, steps, lane, grow):
    rolled = [pltpu.roll(t, steps, 1) for t in tiles]
    outside = jnp.zeros_like(rolled[0])
    result = [jnp.where(lane < steps, outside, rolled[0])]
    for before, after in zip(rolled[:-1], rolled[1:]):
        result.append(jnp.where(lane < steps, before, after))
    if grow:
        result.append(jnp.where(lane < steps, rolled[-1], outside))
    return result


def filter_kernel(x_ref, taps_ref, cos_ref, out_ref, frames_ref, weight_ref, bands_ref):
    step = pl.program_id(0)
    for frame in range(CHUNK):
        row = pl.multiple_of((step * CHUNK + frame) * BLOCK, BLOCK)
        for half in range(2):
            start = frame * BRANCHES + half * LANE
            frames_ref[half, pl.ds(row, BLOCK), :] = x_ref[:, start : start + LANE].astype(
                jnp.float32
            )

    @pl.when(step == pl.num_programs(0) - 1)
    def _():
        table = cos_ref[...]
        for tap in range(TAPS):
            product = table * taps_ref[tap : tap + 1, :].astype(jnp.float32)
            high = product.astype(jnp.bfloat16)
            low = (product - high.astype(jnp.float32)).astype(jnp.bfloat16)
            weight_ref[0, tap * SUBBANDS : (tap + 1) * SUBBANDS, :] = high
            weight_ref[1, tap * SUBBANDS : (tap + 1) * SUBBANDS, :] = low

        lane = lax.broadcasted_iota(jnp.int32, (SUBBANDS, LANE), 1)

        def one_input(i, carry):
            data = jnp.concatenate(
                [frames_ref[half, pl.ds(i, T_DEV, stride=BLOCK), :] for half in range(2)], axis=1
            ).astype(jnp.bfloat16)
            products = nt_dot(weight_ref[0], data) + nt_dot(weight_ref[1], data)
            level = []
            for tap in range(TAPS):
                part = products[tap * SUBBANDS : (tap + 1) * SUBBANDS]
                level.append([part[:, :LANE], part[:, LANE:]])
            steps = 1
            while len(level) > 1:
                merged = []
                for first, second in zip(level[0::2], level[1::2]):
                    moved = shift_lanes(first, steps, lane, grow=len(first) == 2)
                    total = [m + s for m, s in zip(moved, second)]
                    merged.append(total + moved[len(second) :])
                level = merged
                steps *= 2
            for tile, value in enumerate(level[0]):
                bands_ref[tile, pl.ds(i, SUBBANDS, stride=BLOCK), :] = value
            return carry

        lax.fori_loop(0, BLOCK, one_input, 0, unroll=2)
        for tile in range(3):
            out_ref[:, :, tile * LANE : (tile + 1) * LANE] = (
                bands_ref[tile].reshape(SUBBANDS, BLOCK, LANE).astype(jnp.bfloat16)
            )


def filter_bank(samples, taps, table):
    steps = T_DEV // CHUNK
    return pl.pallas_call(
        filter_kernel,
        grid=(steps,),
        in_specs=[
            pl.BlockSpec((BLOCK, CHUNK * BRANCHES), lambda c: (0, c)),
            pl.BlockSpec((TAPS, BRANCHES), lambda c: (0, 0)),
            pl.BlockSpec((SUBBANDS, BRANCHES), lambda c: (0, 0)),
        ],
        out_specs=pl.BlockSpec((SUBBANDS, BLOCK, T_DEV + TAIL), lambda c: (0, 0, 0)),
        out_shape=jax.ShapeDtypeStruct((SUBBANDS, BLOCK, T_DEV + TAIL), jnp.bfloat16),
        scratch_shapes=[
            pltpu.VMEM((2, T_DEV * BLOCK, LANE), jnp.float32),
            pltpu.VMEM((2, TAPS * SUBBANDS, BRANCHES), jnp.bfloat16),
            pltpu.VMEM((3, SUBBANDS * BLOCK, LANE), jnp.float32),
        ],
        compiler_params=pltpu.CompilerParams(vmem_limit_bytes=32 << 20),
        name="filter_bank",
    )(samples, taps, table)


def assemble_kernel(parts_ref, out_ref):
    for core in range(2):
        rows = slice(core * BLOCK, (core + 1) * BLOCK)
        for block in range(N_SUB):
            here = parts_ref[block * 2 + core]
            start = block * T_DEV
            head = here[:, :LANE]
            if block:
                tail = parts_ref[(block - 1) * 2 + core][:, T_DEV:]
                head = (head.astype(jnp.float32) + tail.astype(jnp.float32)).astype(jnp.bfloat16)
            out_ref[rows, start : start + LANE] = head
            out_ref[rows, start + LANE : start + T_DEV] = here[:, LANE:T_DEV]


def assemble(parts):
    return pl.pallas_call(
        assemble_kernel,
        out_shape=jax.ShapeDtypeStruct((2 * BLOCK, TOTAL), jnp.bfloat16),
        name="assemble",
    )(parts)


PAIRS = 4
SPAN = 9 * BLOCK


def build_rows(own_ref, target_ref, slot, first, mask):
    for a in range(2):
        before = None
        for tile in range(TOTAL // LANE + 1):
            row = own_ref[tile, pl.ds(first + a, 1), :]
            rolled = pltpu.roll(
                jnp.broadcast_to(row, (LAGS, LANE)), 0, 1, stride=1, stride_axis=0
            )
            if tile:
                target_ref[slot, a * LAGS : (a + 1) * LAGS, (tile - 1) * LANE : tile * LANE] = (
                    jnp.where(mask, rolled, before).astype(jnp.bfloat16)
                )
            before = rolled


def correlate_kernel(where_ref, *refs):
    blocks = refs[: REACH + 1]
    out_ref, own_ref, span_ref, rows_ref = refs[-4:]
    step = pl.program_id(0)
    row = lax.broadcasted_iota(jnp.int32, (LAGS, LANE), 0)
    mask = lax.broadcasted_iota(jnp.int32, (LAGS, LANE), 1) >= row
    core = where_ref[0]

    @pl.when(step == 0)
    def _():
        offset = pl.multiple_of(core * BLOCK, BLOCK)
        for j in range(REACH + 1):
            size = BLOCK if j == REACH else 2 * BLOCK
            start = 2 * BLOCK * j

            @pl.when(core == 0)
            def _():
                span_ref[start : start + size, :] = blocks[j][:size, :]

            @pl.when(core == 1)
            def _():
                if j == 0:
                    span_ref[:BLOCK, :] = blocks[j][BLOCK:, :]
                else:
                    span_ref[start - BLOCK : start + BLOCK, :] = blocks[j][...]

        own = span_ref[:BLOCK, :].astype(jnp.float32)
        half = jnp.zeros((BLOCK, LAGS // 2), jnp.float32)
        padded = jnp.concatenate([half, own, half], axis=1)
        for tile in range(TOTAL // LANE + 1):
            own_ref[tile] = padded[:, tile * LANE : (tile + 1) * LANE]
        build_rows(own_ref, rows_ref, 0, 0, mask)

    scale = 1.0 / math.sqrt(TOTAL)
    for pair in range(PAIRS):
        index = step * PAIRS + pair
        result = nt_dot(span_ref[...], rows_ref[pair % 2]) * scale
        following = jnp.minimum(index + 1, BLOCK // 2 - 1)
        build_rows(own_ref, rows_ref, (pair + 1) % 2, 2 * following, mask)
        out_ref[0, 2 * pair] = result[:, :LAGS].astype(jnp.bfloat16)
        out_ref[0, 2 * pair + 1] = result[:, LAGS:].astype(jnp.bfloat16)


def correlate(where, blocks, earlier):
    steps = BLOCK // (2 * PAIRS)
    operands = list(blocks)
    in_specs = [pl.BlockSpec((2 * BLOCK, TOTAL), lambda c, w: (0, 0)) for _ in blocks]
    aliases = {}
    if earlier is not None:
        operands.append(earlier)
        in_specs.append(pl.BlockSpec(memory_space=pl.ANY))
        aliases = {len(operands): 0}
    return pl.pallas_call(
        correlate_kernel,
        grid_spec=pltpu.PrefetchScalarGridSpec(
            num_scalar_prefetch=1,
            grid=(steps,),
            in_specs=in_specs,
            out_specs=pl.BlockSpec(
                (1, 2 * PAIRS, SPAN, LAGS), lambda c, w: (w[1], c, 0, 0)
            ),
            scratch_shapes=[
                pltpu.VMEM((TOTAL // LANE + 1, BLOCK, LANE), jnp.float32),
                pltpu.VMEM((SPAN, TOTAL), jnp.bfloat16),
                pltpu.VMEM((2, 2 * LAGS, TOTAL), jnp.bfloat16),
            ],
        ),
        out_shape=jax.ShapeDtypeStruct((2, BLOCK, SPAN, LAGS), jnp.bfloat16),
        input_output_aliases=aliases,
        compiler_params=pltpu.CompilerParams(vmem_limit_bytes=32 << 20),
        name="correlate",
        cost_estimate=pl.CostEstimate(
            flops=2 * BLOCK * SPAN * LAGS * TOTAL, bytes_accessed=4 << 20, transcendentals=0
        ),
    )(where, *operands)


def body(samples, taps):
    core = lax.axis_index("core")
    parts = filter_bank(samples, taps.reshape(TAPS, BRANCHES), cosine_matrix())
    parts = lax.all_to_all(parts, ("sub", "core"), split_axis=0, concat_axis=0, tiled=True)
    mine = assemble(parts)
    held = [mine]
    for step in range(1, REACH + 1):
        pairs = [(source, (source - step) % CHIPS) for source in range(CHIPS)]
        held.append(lax.ppermute(mine, "chip", pairs))
    swapped = [lax.ppermute(value, "core", [(0, 1), (1, 0)]) for value in held]
    first = correlate(jnp.stack([core, core]), held, None)
    return correlate(jnp.stack([core, 1 - core]), swapped, first)


def solution(mesh):
    inner = Mesh(mesh.devices.reshape(N_SUB, CHIPS, 2), ("sub", "chip", "core"))
    in_specs = (P(("chip", "core"), "sub"), P())
    out_specs = P("sub", ("chip", "core"), None, None)
    return jax.shard_map(body, mesh=inner, in_specs=in_specs, out_specs=out_specs, check_vma=False)
```

```python
import functools
import math

import jax
import jax.numpy as jnp
import numpy as np
from jax import lax
from jax.experimental import pallas as pl
from jax.experimental.pallas import tpu as pltpu
from jax.sharding import Mesh
from jax.sharding import PartitionSpec as P

BRANCHES = 256
TAPS = 16
LAGS = 128
T_DEV = 256
SUBBANDS = 16
BLOCK = 32
N_SUB = 8
CHIPS = 8
TOTAL = T_DEV * N_SUB
TAIL = 128
CHUNK = 32
REACH = 4
LANE = 128
PITCH = 40


def cosine_matrix():
    band = np.float32(BRANCHES // 2 - SUBBANDS // 2) + np.arange(SUBBANDS, dtype=np.float32)
    band = band + np.float32(0.5)
    arm = np.arange(BRANCHES, dtype=np.float32) + np.float32(0.5)
    angle = np.float32(math.pi / BRANCHES) * band[:, None] * arm[None, :]
    table = np.cos(angle) * np.float32(math.sqrt(2.0 / BRANCHES) / 512.0)
    return jnp.asarray(table).astype(jnp.bfloat16).astype(jnp.float32)


def nt_dot(a, b):
    return lax.dot_general(a, b, (((1,), (1,)), ((), ())), preferred_element_type=jnp.float32)


def shift_lanes(tiles, steps, lane, grow):
    rolled = [pltpu.roll(t, steps, 1) for t in tiles]
    outside = jnp.zeros_like(rolled[0])
    result = [jnp.where(lane < steps, outside, rolled[0])]
    for before, after in zip(rolled[:-1], rolled[1:]):
        result.append(jnp.where(lane < steps, before, after))
    if grow:
        result.append(jnp.where(lane < steps, rolled[-1], outside))
    return result


def filter_kernel(
    x_hbm, taps_hbm, cos_hbm, out_ref, x_ref, taps_ref, cos_ref, frames_ref, weight_ref, bands_ref, sems
):
    def fetch(c):
        columns = pl.ds(c * CHUNK * BRANCHES, CHUNK * BRANCHES)
        return pltpu.make_async_copy(x_hbm.at[:, columns], x_ref.at[:, columns], sems.at[c])

    chunks = T_DEV // CHUNK
    taps_copy = pltpu.make_async_copy(taps_hbm, taps_ref, sems.at[chunks])
    cos_copy = pltpu.make_async_copy(cos_hbm, cos_ref, sems.at[chunks + 1])
    taps_copy.start()
    cos_copy.start()
    for c in range(chunks):
        fetch(c).start()
    taps_copy.wait()
    cos_copy.wait()
    table = cos_ref[...]
    for tap in range(TAPS):
        coefficients = taps_ref[:, tap * BRANCHES : (tap + 1) * BRANCHES].astype(jnp.float32)
        product = table * coefficients
        high = product.astype(jnp.bfloat16)
        low = (product - high.astype(jnp.float32)).astype(jnp.bfloat16)
        weight_ref[0, tap * SUBBANDS : (tap + 1) * SUBBANDS, :] = high
        weight_ref[1, tap * SUBBANDS : (tap + 1) * SUBBANDS, :] = low

    for c in range(chunks):
        fetch(c).wait()

        def one_frame(frame, carry):
            row = pl.multiple_of(frame * PITCH, 8)
            for half in range(2):
                start = pl.multiple_of(frame * BRANCHES + half * LANE, LANE)
                frames_ref[half, pl.ds(row, BLOCK), :] = x_ref[:, pl.ds(start, LANE)].astype(
                    jnp.float32
                )
            return carry

        lax.fori_loop(c * CHUNK, (c + 1) * CHUNK, one_frame, 0, unroll=8)

    lane = lax.broadcasted_iota(jnp.int32, (SUBBANDS, LANE), 1)

    def one_input(i, carry):
        data = jnp.concatenate(
            [frames_ref[half, pl.ds(i, T_DEV, stride=PITCH), :] for half in range(2)], axis=1
        ).astype(jnp.bfloat16)
        products = nt_dot(weight_ref[0], data) + nt_dot(weight_ref[1], data)
        level = []
        for tap in range(TAPS):
            part = products[tap * SUBBANDS : (tap + 1) * SUBBANDS]
            level.append([part[:, :LANE], part[:, LANE:]])
        steps = 1
        while len(level) > 1:
            merged = []
            for first, second in zip(level[0::2], level[1::2]):
                moved = shift_lanes(first, steps, lane, grow=len(first) == 2)
                total = [m + s for m, s in zip(moved, second)]
                merged.append(total + moved[len(second) :])
            level = merged
            steps *= 2
        for tile, value in enumerate(level[0]):
            bands_ref[tile, pl.ds(i, SUBBANDS, stride=PITCH), :] = value
        return carry

    lax.fori_loop(0, BLOCK, one_input, 0, unroll=16)
    for tile in range(3):
        out_ref[:, :, tile * LANE : (tile + 1) * LANE] = (
            bands_ref[tile].reshape(SUBBANDS, PITCH, LANE)[:, :BLOCK].astype(jnp.bfloat16)
        )


def filter_bank(samples, taps, table):
    return pl.pallas_call(
        filter_kernel,
        in_specs=[pl.BlockSpec(memory_space=pl.ANY)] * 3,
        out_specs=pl.BlockSpec(memory_space=pltpu.VMEM),
        out_shape=jax.ShapeDtypeStruct((SUBBANDS, BLOCK, T_DEV + TAIL), jnp.bfloat16),
        scratch_shapes=[
            pltpu.VMEM((BLOCK, T_DEV * BRANCHES), jnp.bfloat16),
            pltpu.VMEM((1, TAPS * BRANCHES), jnp.int32),
            pltpu.VMEM((SUBBANDS, BRANCHES), jnp.float32),
            pltpu.VMEM((2, T_DEV * PITCH, LANE), jnp.float32),
            pltpu.VMEM((2, TAPS * SUBBANDS, BRANCHES), jnp.bfloat16),
            pltpu.VMEM((3, SUBBANDS * PITCH, LANE), jnp.float32),
            pltpu.SemaphoreType.DMA((T_DEV // CHUNK + 2,)),
        ],
        compiler_params=pltpu.CompilerParams(vmem_limit_bytes=60 << 20),
        name="filter_bank",
    )(samples, taps, table)


def assemble_kernel(parts_ref, out_ref):
    for core in range(2):
        rows = slice(core * BLOCK, (core + 1) * BLOCK)
        for block in range(N_SUB):
            here = parts_ref[block * 2 + core]
            start = block * T_DEV
            head = here[:, :LANE]
            if block:
                tail = parts_ref[(block - 1) * 2 + core][:, T_DEV:]
                head = (head.astype(jnp.float32) + tail.astype(jnp.float32)).astype(jnp.bfloat16)
            out_ref[rows, start : start + LANE] = head
            out_ref[rows, start + LANE : start + T_DEV] = here[:, LANE:T_DEV]


def assemble(parts):
    return pl.pallas_call(
        assemble_kernel,
        out_shape=jax.ShapeDtypeStruct((2 * BLOCK, TOTAL), jnp.bfloat16),
        name="assemble",
    )(parts)


PAIRS = 4
SPAN = 9 * BLOCK


def build_rows(own_ref, target_ref, slot, first, mask):
    for a in range(2):
        before = None
        for tile in range(TOTAL // LANE + 1):
            row = own_ref[tile, pl.ds(first + a, 1), :]
            rolled = pltpu.roll(
                jnp.broadcast_to(row, (LAGS, LANE)), 0, 1, stride=1, stride_axis=0
            )
            if tile:
                target_ref[slot, a * LAGS : (a + 1) * LAGS, (tile - 1) * LANE : tile * LANE] = (
                    jnp.where(mask, rolled, before).astype(jnp.bfloat16)
                )
            before = rolled


def correlate_kernel(where_ref, *refs):
    blocks = refs[: REACH + 1]
    out_ref, own_ref, span_ref, rows_ref = refs[-4:]
    step = pl.program_id(0)
    row = lax.broadcasted_iota(jnp.int32, (LAGS, LANE), 0)
    mask = lax.broadcasted_iota(jnp.int32, (LAGS, LANE), 1) >= row
    core = where_ref[0]

    @pl.when(step == 0)
    def _():
        offset = pl.multiple_of(core * BLOCK, BLOCK)
        for j in range(REACH + 1):
            size = BLOCK if j == REACH else 2 * BLOCK
            start = 2 * BLOCK * j

            @pl.when(core == 0)
            def _():
                span_ref[start : start + size, :] = blocks[j][:size, :]

            @pl.when(core == 1)
            def _():
                if j == 0:
                    span_ref[:BLOCK, :] = blocks[j][BLOCK:, :]
                else:
                    span_ref[start - BLOCK : start + BLOCK, :] = blocks[j][...]

        own = span_ref[:BLOCK, :].astype(jnp.float32)
        half = jnp.zeros((BLOCK, LAGS // 2), jnp.float32)
        padded = jnp.concatenate([half, own, half], axis=1)
        for tile in range(TOTAL // LANE + 1):
            own_ref[tile] = padded[:, tile * LANE : (tile + 1) * LANE]
        build_rows(own_ref, rows_ref, 0, 0, mask)

    scale = 1.0 / math.sqrt(TOTAL)
    for pair in range(PAIRS):
        index = step * PAIRS + pair
        result = nt_dot(span_ref[...], rows_ref[pair % 2]) * scale
        following = jnp.minimum(index + 1, BLOCK // 2 - 1)
        build_rows(own_ref, rows_ref, (pair + 1) % 2, 2 * following, mask)
        out_ref[0, 2 * pair] = result[:, :LAGS].astype(jnp.bfloat16)
        out_ref[0, 2 * pair + 1] = result[:, LAGS:].astype(jnp.bfloat16)


def correlate(where, blocks, earlier):
    steps = BLOCK // (2 * PAIRS)
    operands = list(blocks)
    in_specs = [pl.BlockSpec((2 * BLOCK, TOTAL), lambda c, w: (0, 0)) for _ in blocks]
    aliases = {}
    if earlier is not None:
        operands.append(earlier)
        in_specs.append(pl.BlockSpec(memory_space=pl.ANY))
        aliases = {len(operands): 0}
    return pl.pallas_call(
        correlate_kernel,
        grid_spec=pltpu.PrefetchScalarGridSpec(
            num_scalar_prefetch=1,
            grid=(steps,),
            in_specs=in_specs,
            out_specs=pl.BlockSpec(
                (1, 2 * PAIRS, SPAN, LAGS), lambda c, w: (w[1], c, 0, 0)
            ),
            scratch_shapes=[
                pltpu.VMEM((TOTAL // LANE + 1, BLOCK, LANE), jnp.float32),
                pltpu.VMEM((SPAN, TOTAL), jnp.bfloat16),
                pltpu.VMEM((2, 2 * LAGS, TOTAL), jnp.bfloat16),
            ],
        ),
        out_shape=jax.ShapeDtypeStruct((2, BLOCK, SPAN, LAGS), jnp.bfloat16),
        input_output_aliases=aliases,
        compiler_params=pltpu.CompilerParams(vmem_limit_bytes=32 << 20),
        name="correlate",
        cost_estimate=pl.CostEstimate(
            flops=2 * BLOCK * SPAN * LAGS * TOTAL, bytes_accessed=4 << 20, transcendentals=0
        ),
    )(where, *operands)


def body(samples, taps):
    core = lax.axis_index("core")
    parts = filter_bank(samples, taps[None], cosine_matrix())
    parts = lax.all_to_all(parts, ("sub", "core"), split_axis=0, concat_axis=0, tiled=True)
    mine = assemble(parts)
    held = [mine]
    for step in range(1, REACH + 1):
        pairs = [(source, (source - step) % CHIPS) for source in range(CHIPS)]
        held.append(lax.ppermute(mine, "chip", pairs))
    swapped = [lax.ppermute(value, "core", [(0, 1), (1, 0)]) for value in held]
    first = correlate(jnp.stack([core, core]), held, None)
    return correlate(jnp.stack([core, 1 - core]), swapped, first)


def solution(mesh):
    inner = Mesh(mesh.devices.reshape(N_SUB, CHIPS, 2), ("sub", "chip", "core"))
    in_specs = (P(("chip", "core"), "sub"), P())
    out_specs = P("sub", ("chip", "core"), None, None)
    return jax.shard_map(body, mesh=inner, in_specs=in_specs, out_specs=out_specs, check_vma=False)
```

```python
import functools
import math

import jax
import jax.numpy as jnp
import numpy as np
from jax import lax
from jax.experimental import pallas as pl
from jax.experimental.pallas import tpu as pltpu
from jax.sharding import Mesh
from jax.sharding import PartitionSpec as P

BRANCHES = 256
TAPS = 16
LAGS = 128
T_DEV = 256
SUBBANDS = 16
BLOCK = 32
N_SUB = 8
ROWS = 4
TOTAL = T_DEV * N_SUB
TAIL = 128
CHUNK = 32
REACH = 4
LANE = 128
PITCH = 40


def cosine_matrix():
    band = np.float32(BRANCHES // 2 - SUBBANDS // 2) + np.arange(SUBBANDS, dtype=np.float32)
    band = band + np.float32(0.5)
    arm = np.arange(BRANCHES, dtype=np.float32) + np.float32(0.5)
    angle = np.float32(math.pi / BRANCHES) * band[:, None] * arm[None, :]
    table = np.cos(angle) * np.float32(math.sqrt(2.0 / BRANCHES) / 512.0)
    return jnp.asarray(table).astype(jnp.bfloat16).astype(jnp.float32)


def nt_dot(a, b):
    return lax.dot_general(a, b, (((1,), (1,)), ((), ())), preferred_element_type=jnp.float32)


def shift_lanes(tiles, steps, lane, grow):
    rolled = [pltpu.roll(t, steps, 1) for t in tiles]
    outside = jnp.zeros_like(rolled[0])
    result = [jnp.where(lane < steps, outside, rolled[0])]
    for before, after in zip(rolled[:-1], rolled[1:]):
        result.append(jnp.where(lane < steps, before, after))
    if grow:
        result.append(jnp.where(lane < steps, rolled[-1], outside))
    return result


def filter_kernel(
    x_hbm, taps_hbm, cos_hbm, out_ref, x_ref, taps_ref, cos_ref, frames_ref, weight_ref, bands_ref, sems
):
    def fetch(c):
        columns = pl.ds(c * CHUNK * BRANCHES, CHUNK * BRANCHES)
        return pltpu.make_async_copy(x_hbm.at[:, columns], x_ref.at[:, columns], sems.at[c])

    chunks = T_DEV // CHUNK
    taps_copy = pltpu.make_async_copy(taps_hbm, taps_ref, sems.at[chunks])
    cos_copy = pltpu.make_async_copy(cos_hbm, cos_ref, sems.at[chunks + 1])
    taps_copy.start()
    cos_copy.start()
    for c in range(chunks):
        fetch(c).start()
    taps_copy.wait()
    cos_copy.wait()
    table = cos_ref[...]
    for tap in range(TAPS):
        coefficients = taps_ref[:, tap * BRANCHES : (tap + 1) * BRANCHES].astype(jnp.float32)
        product = table * coefficients
        high = product.astype(jnp.bfloat16)
        low = (product - high.astype(jnp.float32)).astype(jnp.bfloat16)
        weight_ref[0, tap * SUBBANDS : (tap + 1) * SUBBANDS, :] = high
        weight_ref[1, tap * SUBBANDS : (tap + 1) * SUBBANDS, :] = low

    for c in range(chunks):
        fetch(c).wait()

        def one_frame(frame, carry):
            row = pl.multiple_of(frame * PITCH, 8)
            for half in range(2):
                start = pl.multiple_of(frame * BRANCHES + half * LANE, LANE)
                frames_ref[half, pl.ds(row, BLOCK), :] = x_ref[:, pl.ds(start, LANE)].astype(
                    jnp.float32
                )
            return carry

        lax.fori_loop(c * CHUNK, (c + 1) * CHUNK, one_frame, 0, unroll=8)

    lane = lax.broadcasted_iota(jnp.int32, (SUBBANDS, LANE), 1)

    def one_input(i, carry):
        data = jnp.concatenate(
            [frames_ref[half, pl.ds(i, T_DEV, stride=PITCH), :] for half in range(2)], axis=1
        ).astype(jnp.bfloat16)
        products = nt_dot(weight_ref[0], data) + nt_dot(weight_ref[1], data)
        level = []
        for tap in range(TAPS):
            part = products[tap * SUBBANDS : (tap + 1) * SUBBANDS]
            level.append([part[:, :LANE], part[:, LANE:]])
        steps = 1
        while len(level) > 1:
            merged = []
            for first, second in zip(level[0::2], level[1::2]):
                moved = shift_lanes(first, steps, lane, grow=len(first) == 2)
                total = [m + s for m, s in zip(moved, second)]
                merged.append(total + moved[len(second) :])
            level = merged
            steps *= 2
        for tile, value in enumerate(level[0]):
            bands_ref[tile, pl.ds(i, SUBBANDS, stride=PITCH), :] = value
        return carry

    lax.fori_loop(0, BLOCK, one_input, 0, unroll=16)
    for tile in range(3):
        out_ref[:, :, tile * LANE : (tile + 1) * LANE] = (
            bands_ref[tile].reshape(SUBBANDS, PITCH, LANE)[:, :BLOCK].astype(jnp.bfloat16)
        )


def filter_bank(samples, taps, table):
    return pl.pallas_call(
        filter_kernel,
        in_specs=[pl.BlockSpec(memory_space=pl.ANY)] * 3,
        out_specs=pl.BlockSpec(memory_space=pltpu.VMEM),
        out_shape=jax.ShapeDtypeStruct((SUBBANDS, BLOCK, T_DEV + TAIL), jnp.bfloat16),
        scratch_shapes=[
            pltpu.VMEM((BLOCK, T_DEV * BRANCHES), jnp.bfloat16),
            pltpu.VMEM((1, TAPS * BRANCHES), jnp.int32),
            pltpu.VMEM((SUBBANDS, BRANCHES), jnp.float32),
            pltpu.VMEM((2, T_DEV * PITCH, LANE), jnp.float32),
            pltpu.VMEM((2, TAPS * SUBBANDS, BRANCHES), jnp.bfloat16),
            pltpu.VMEM((3, SUBBANDS * PITCH, LANE), jnp.float32),
            pltpu.SemaphoreType.DMA((T_DEV // CHUNK + 2,)),
        ],
        compiler_params=pltpu.CompilerParams(vmem_limit_bytes=60 << 20),
        name="filter_bank",
    )(samples, taps, table)


def assemble_kernel(parts_ref, out_ref):
    for core in range(2):
        rows = slice(core * BLOCK, (core + 1) * BLOCK)
        for block in range(N_SUB):
            here = parts_ref[block * 2 + core]
            start = block * T_DEV
            head = here[:, :LANE]
            if block:
                tail = parts_ref[(block - 1) * 2 + core][:, T_DEV:]
                head = (head.astype(jnp.float32) + tail.astype(jnp.float32)).astype(jnp.bfloat16)
            out_ref[rows, start : start + LANE] = head
            out_ref[rows, start + LANE : start + T_DEV] = here[:, LANE:T_DEV]


def assemble(parts):
    return pl.pallas_call(
        assemble_kernel,
        out_shape=jax.ShapeDtypeStruct((2 * BLOCK, TOTAL), jnp.bfloat16),
        name="assemble",
    )(parts)


PAIRS = 8
SPAN = 9 * BLOCK


def build_rows(own_ref, target_ref, slot, first, mask):
    for a in range(2):
        before = None
        for tile in range(TOTAL // LANE + 1):
            row = own_ref[tile, pl.ds(first + a, 1), :]
            rolled = pltpu.roll(
                jnp.broadcast_to(row, (LAGS, LANE)), 0, 1, stride=1, stride_axis=0
            )
            if tile:
                target_ref[slot, a * LAGS : (a + 1) * LAGS, (tile - 1) * LANE : tile * LANE] = (
                    jnp.where(mask, rolled, before).astype(jnp.bfloat16)
                )
            before = rolled


HELD = 6


def chip_source(j, column):
    return {1: (3, 4), 2: (1, 1), 3: (4, 5), 4: (2, 2)}[j][column]


def correlate_kernel(core_ref, column_ref, *refs):
    count = HELD
    straight, crossed = refs[:count], refs[count : 2 * count]
    out_ref, own_ref, span_ref, rows_ref, mine_ref, sems = refs[2 * count :]
    band = pl.program_id(0)
    step = pl.program_id(1)
    row = lax.broadcasted_iota(jnp.int32, (LAGS, LANE), 0)
    mask = lax.broadcasted_iota(jnp.int32, (LAGS, LANE), 1) >= row
    core = core_ref[0]
    column = column_ref[0]

    def gather(blocks, base):
        first = pltpu.make_async_copy(base, mine_ref, sems.at[0])
        first.start()
        for j in range(1, REACH + 1):
            size = BLOCK if j == REACH else 2 * BLOCK
            start = 2 * BLOCK * j

            columns = {}
            for number in range(2):
                columns.setdefault(chip_source(j, number), []).append(number)
            for source, which in columns.items():
                here = (column >= which[0]) & (column <= which[-1])

                @pl.when(here & (core == 0))
                def _():
                    span_ref[start : start + size, :] = blocks[source][:size, :]

                @pl.when(here & (core == 1))
                def _():
                    span_ref[start - BLOCK : start + BLOCK, :] = blocks[source][...]

        first.wait()

        @pl.when(core == 0)
        def _():
            span_ref[: 2 * BLOCK, :] = mine_ref[...]

        @pl.when(core == 1)
        def _():
            span_ref[:BLOCK, :] = mine_ref[BLOCK:, :]

        own = span_ref[:BLOCK, :].astype(jnp.float32)
        half = jnp.zeros((BLOCK, LAGS // 2), jnp.float32)
        padded = jnp.concatenate([half, own, half], axis=1)
        for tile in range(TOTAL // LANE + 1):
            own_ref[tile] = padded[:, tile * LANE : (tile + 1) * LANE]
        build_rows(own_ref, rows_ref, 0, 0, mask)

    @pl.when(jnp.logical_and(step == 0, band == 0))
    def _():
        gather(straight, straight[0])

    @pl.when(jnp.logical_and(step == 0, band == 1))
    def _():
        gather(crossed, crossed[0])

    scale = 1.0 / math.sqrt(TOTAL)
    for pair in range(PAIRS):
        index = step * PAIRS + pair
        result = nt_dot(span_ref[...], rows_ref[pair % 2]) * scale
        following = jnp.minimum(index + 1, BLOCK // 2 - 1)
        build_rows(own_ref, rows_ref, (pair + 1) % 2, 2 * following, mask)
        out_ref[0, 2 * pair] = result[:, :LAGS].astype(jnp.bfloat16)
        out_ref[0, 2 * pair + 1] = result[:, LAGS:].astype(jnp.bfloat16)


def correlate(core, column, straight, crossed):
    steps = BLOCK // (2 * PAIRS)
    held = pl.BlockSpec(memory_space=pltpu.VMEM)
    anywhere = pl.BlockSpec(memory_space=pl.ANY)
    return pl.pallas_call(
        correlate_kernel,
        grid_spec=pltpu.PrefetchScalarGridSpec(
            num_scalar_prefetch=2,
            grid=(2, steps),
            in_specs=([anywhere] + [held] * (HELD - 1)) * 2,
            out_specs=pl.BlockSpec(
                (1, 2 * PAIRS, SPAN, LAGS), lambda s, c, w, v: (lax.rem(w[0] + s, 2), c, 0, 0)
            ),
            scratch_shapes=[
                pltpu.VMEM((TOTAL // LANE + 1, BLOCK, LANE), jnp.float32),
                pltpu.VMEM((SPAN, TOTAL), jnp.bfloat16),
                pltpu.VMEM((2, 2 * LAGS, TOTAL), jnp.bfloat16),
                pltpu.VMEM((2 * BLOCK, TOTAL), jnp.bfloat16),
                pltpu.SemaphoreType.DMA((1,)),
            ],
        ),
        out_shape=jax.ShapeDtypeStruct((2, BLOCK, SPAN, LAGS), jnp.bfloat16),
        compiler_params=pltpu.CompilerParams(vmem_limit_bytes=32 << 20),
        name="correlate",
        cost_estimate=pl.CostEstimate(
            flops=4 * BLOCK * SPAN * LAGS * TOTAL, bytes_accessed=8 << 20, transcendentals=0
        ),
    )(core, column, *straight, *crossed)


def up(value, steps):
    pairs = [(source, (source - steps) % ROWS) for source in range(ROWS)]
    return lax.ppermute(value, "row", pairs)


def body(samples, taps):
    core = lax.axis_index("core")
    parts = filter_bank(samples, taps[None], cosine_matrix())
    parts = lax.all_to_all(parts, ("sub", "core"), split_axis=0, concat_axis=0, tiled=True)
    mine = assemble(parts)
    above, second = up(mine, 1), up(mine, 2)
    held = [
        mine,
        above,
        second,
        lax.ppermute(mine, "column", [(1, 0)]),
        lax.ppermute(above, "column", [(0, 1), (1, 0)]),
        lax.ppermute(second, "column", [(0, 1)]),
    ]
    swapped = [lax.ppermute(value, "core", [(0, 1), (1, 0)]) for value in held]
    column = lax.axis_index("column")
    return correlate(core[None], column[None], held, swapped)


def solution(mesh):
    inner = Mesh(mesh.devices.reshape(N_SUB, ROWS, 2, 2), ("sub", "row", "column", "core"))
    stations = ("row", "column", "core")
    in_specs = (P(stations, "sub"), P())
    out_specs = P("sub", stations, None, None)
    return jax.shard_map(body, mesh=inner, in_specs=in_specs, out_specs=out_specs, check_vma=False)
```

```python
import functools
import math

import jax
import jax.numpy as jnp
import numpy as np
from jax import lax
from jax.experimental import pallas as pl
from jax.experimental.pallas import tpu as pltpu
from jax.sharding import Mesh
from jax.sharding import PartitionSpec as P

BRANCHES = 256
TAPS = 16
LAGS = 128
T_DEV = 256
SUBBANDS = 16
BLOCK = 32
N_SUB = 8
ROWS = 4
TOTAL = T_DEV * N_SUB
TAIL = 128
CHUNK = 32
REACH = 4
LANE = 128
PITCH = 40


def cosine_matrix():
    band = np.float32(BRANCHES // 2 - SUBBANDS // 2) + np.arange(SUBBANDS, dtype=np.float32)
    band = band + np.float32(0.5)
    arm = np.arange(BRANCHES, dtype=np.float32) + np.float32(0.5)
    angle = np.float32(math.pi / BRANCHES) * band[:, None] * arm[None, :]
    table = np.cos(angle) * np.float32(math.sqrt(2.0 / BRANCHES) / 512.0)
    return jnp.asarray(table).astype(jnp.bfloat16).astype(jnp.float32)


def nt_dot(a, b):
    return lax.dot_general(a, b, (((1,), (1,)), ((), ())), preferred_element_type=jnp.float32)


def shift_lanes(tiles, steps, lane, grow):
    rolled = [pltpu.roll(t, steps, 1) for t in tiles]
    outside = jnp.zeros_like(rolled[0])
    result = [jnp.where(lane < steps, outside, rolled[0])]
    for before, after in zip(rolled[:-1], rolled[1:]):
        result.append(jnp.where(lane < steps, before, after))
    if grow:
        result.append(jnp.where(lane < steps, rolled[-1], outside))
    return result


def filter_kernel(
    x_hbm, taps_hbm, cos_hbm, out_ref, x_ref, taps_ref, cos_ref, frames_ref, weight_ref, bands_ref, sems
):
    def fetch(c):
        columns = pl.ds(c * CHUNK * BRANCHES, CHUNK * BRANCHES)
        return pltpu.make_async_copy(x_hbm.at[:, columns], x_ref.at[:, columns], sems.at[c])

    chunks = T_DEV // CHUNK
    taps_copy = pltpu.make_async_copy(taps_hbm, taps_ref, sems.at[chunks])
    cos_copy = pltpu.make_async_copy(cos_hbm, cos_ref, sems.at[chunks + 1])
    taps_copy.start()
    cos_copy.start()
    for c in range(chunks):
        fetch(c).start()
    taps_copy.wait()
    cos_copy.wait()
    table = cos_ref[...]
    for tap in range(TAPS):
        coefficients = taps_ref[:, tap * BRANCHES : (tap + 1) * BRANCHES].astype(jnp.float32)
        product = table * coefficients
        high = product.astype(jnp.bfloat16)
        low = (product - high.astype(jnp.float32)).astype(jnp.bfloat16)
        weight_ref[0, tap * SUBBANDS : (tap + 1) * SUBBANDS, :] = high
        weight_ref[1, tap * SUBBANDS : (tap + 1) * SUBBANDS, :] = low

    for c in range(chunks):
        fetch(c).wait()

        def one_frame(frame, carry):
            row = pl.multiple_of(frame * PITCH, 8)
            for half in range(2):
                start = pl.multiple_of(frame * BRANCHES + half * LANE, LANE)
                frames_ref[half, pl.ds(row, BLOCK), :] = x_ref[:, pl.ds(start, LANE)].astype(
                    jnp.float32
                )
            return carry

        lax.fori_loop(c * CHUNK, (c + 1) * CHUNK, one_frame, 0, unroll=8)

    lane = lax.broadcasted_iota(jnp.int32, (SUBBANDS, LANE), 1)

    def one_input(i, carry):
        data = jnp.concatenate(
            [frames_ref[half, pl.ds(i, T_DEV, stride=PITCH), :] for half in range(2)], axis=1
        ).astype(jnp.bfloat16)
        products = nt_dot(weight_ref[0], data) + nt_dot(weight_ref[1], data)
        level = []
        for tap in range(TAPS):
            part = products[tap * SUBBANDS : (tap + 1) * SUBBANDS]
            level.append([part[:, :LANE], part[:, LANE:]])
        steps = 1
        while len(level) > 1:
            merged = []
            for first, second in zip(level[0::2], level[1::2]):
                moved = shift_lanes(first, steps, lane, grow=len(first) == 2)
                total = [m + s for m, s in zip(moved, second)]
                merged.append(total + moved[len(second) :])
            level = merged
            steps *= 2
        for tile, value in enumerate(level[0]):
            bands_ref[tile, pl.ds(i, SUBBANDS, stride=PITCH), :] = value
        return carry

    lax.fori_loop(0, BLOCK, one_input, 0, unroll=16)
    for tile in range(3):
        out_ref[:, :, tile * LANE : (tile + 1) * LANE] = (
            bands_ref[tile].reshape(SUBBANDS, PITCH, LANE)[:, :BLOCK].astype(jnp.bfloat16)
        )


def filter_bank(samples, taps, table):
    return pl.pallas_call(
        filter_kernel,
        in_specs=[pl.BlockSpec(memory_space=pl.ANY)] * 3,
        out_specs=pl.BlockSpec(memory_space=pltpu.VMEM),
        out_shape=jax.ShapeDtypeStruct((SUBBANDS, BLOCK, T_DEV + TAIL), jnp.bfloat16),
        scratch_shapes=[
            pltpu.VMEM((BLOCK, T_DEV * BRANCHES), jnp.bfloat16),
            pltpu.VMEM((1, TAPS * BRANCHES), jnp.int32),
            pltpu.VMEM((SUBBANDS, BRANCHES), jnp.float32),
            pltpu.VMEM((2, T_DEV * PITCH, LANE), jnp.float32),
            pltpu.VMEM((2, TAPS * SUBBANDS, BRANCHES), jnp.bfloat16),
            pltpu.VMEM((3, SUBBANDS * PITCH, LANE), jnp.float32),
            pltpu.SemaphoreType.DMA((T_DEV // CHUNK + 2,)),
        ],
        compiler_params=pltpu.CompilerParams(vmem_limit_bytes=60 << 20),
        name="filter_bank",
    )(samples, taps, table)


def assemble_kernel(parts_ref, out_ref):
    for core in range(2):
        rows = slice(core * BLOCK, (core + 1) * BLOCK)
        for block in range(N_SUB):
            here = parts_ref[block * 2 + core]
            start = block * T_DEV
            head = here[:, :LANE]
            if block:
                tail = parts_ref[(block - 1) * 2 + core][:, T_DEV:]
                head = (head.astype(jnp.float32) + tail.astype(jnp.float32)).astype(jnp.bfloat16)
            out_ref[rows, start : start + LANE] = head
            out_ref[rows, start + LANE : start + T_DEV] = here[:, LANE:T_DEV]


def assemble(parts):
    return pl.pallas_call(
        assemble_kernel,
        out_shape=jax.ShapeDtypeStruct((2 * BLOCK, TOTAL), jnp.bfloat16),
        name="assemble",
    )(parts)


PAIRS = 8
SPAN = 9 * BLOCK


def build_rows(own_ref, target_ref, slot, first, mask):
    for a in range(2):
        before = None
        for tile in range(TOTAL // LANE + 1):
            row = own_ref[tile, pl.ds(first + a, 1), :]
            rolled = pltpu.roll(
                jnp.broadcast_to(row, (LAGS, LANE)), 0, 1, stride=1, stride_axis=0
            )
            if tile:
                target_ref[slot, a * LAGS : (a + 1) * LAGS, (tile - 1) * LANE : tile * LANE] = (
                    jnp.where(mask, rolled, before).astype(jnp.bfloat16)
                )
            before = rolled


HELD = 6


def chip_source(j, column):
    return {1: (3, 4), 2: (1, 1), 3: (4, 5), 4: (2, 2)}[j][column]


def correlate_kernel(core_ref, column_ref, *refs):
    count = HELD
    straight, crossed = refs[:count], refs[count : 2 * count]
    out_ref, own_ref, span_ref, rows_ref = refs[2 * count :]
    band = pl.program_id(0)
    step = pl.program_id(1)
    row = lax.broadcasted_iota(jnp.int32, (LAGS, LANE), 0)
    mask = lax.broadcasted_iota(jnp.int32, (LAGS, LANE), 1) >= row
    core = core_ref[0]
    column = column_ref[0]

    def gather(blocks):
        for j in range(1, REACH + 1):
            size = BLOCK if j == REACH else 2 * BLOCK
            start = 2 * BLOCK * j

            columns = {}
            for number in range(2):
                columns.setdefault(chip_source(j, number), []).append(number)
            for source, which in columns.items():
                here = (column >= which[0]) & (column <= which[-1])

                @pl.when(here & (core == 0))
                def _():
                    span_ref[start : start + size, :] = blocks[source][:size, :]

                @pl.when(here & (core == 1))
                def _():
                    span_ref[start - BLOCK : start + BLOCK, :] = blocks[source][...]

        @pl.when(core == 0)
        def _():
            span_ref[: 2 * BLOCK, :] = blocks[0][...]

        @pl.when(core == 1)
        def _():
            span_ref[:BLOCK, :] = blocks[0][BLOCK:, :]

        own = span_ref[:BLOCK, :].astype(jnp.float32)
        half = jnp.zeros((BLOCK, LAGS // 2), jnp.float32)
        padded = jnp.concatenate([half, own, half], axis=1)
        for tile in range(TOTAL // LANE + 1):
            own_ref[tile] = padded[:, tile * LANE : (tile + 1) * LANE]
        build_rows(own_ref, rows_ref, 0, 0, mask)

    @pl.when(jnp.logical_and(step == 0, band == 0))
    def _():
        gather(straight)

    @pl.when(jnp.logical_and(step == 0, band == 1))
    def _():
        gather(crossed)

    scale = 1.0 / math.sqrt(TOTAL)
    for pair in range(PAIRS):
        index = step * PAIRS + pair
        result = nt_dot(span_ref[...], rows_ref[pair % 2]) * scale
        following = jnp.minimum(index + 1, BLOCK // 2 - 1)
        build_rows(own_ref, rows_ref, (pair + 1) % 2, 2 * following, mask)
        out_ref[0, 2 * pair] = result[:, :LAGS].astype(jnp.bfloat16)
        out_ref[0, 2 * pair + 1] = result[:, LAGS:].astype(jnp.bfloat16)


def correlate(core, column, straight, crossed):
    steps = BLOCK // (2 * PAIRS)
    held = pl.BlockSpec(memory_space=pltpu.VMEM)
    return pl.pallas_call(
        correlate_kernel,
        grid_spec=pltpu.PrefetchScalarGridSpec(
            num_scalar_prefetch=2,
            grid=(2, steps),
            in_specs=[held] * (2 * HELD),
            out_specs=pl.BlockSpec(
                (1, 2 * PAIRS, SPAN, LAGS), lambda s, c, w, v: (lax.rem(w[0] + s, 2), c, 0, 0)
            ),
            scratch_shapes=[
                pltpu.VMEM((TOTAL // LANE + 1, BLOCK, LANE), jnp.float32),
                pltpu.VMEM((SPAN, TOTAL), jnp.bfloat16),
                pltpu.VMEM((2, 2 * LAGS, TOTAL), jnp.bfloat16),
            ],
        ),
        out_shape=jax.ShapeDtypeStruct((2, BLOCK, SPAN, LAGS), jnp.bfloat16),
        compiler_params=pltpu.CompilerParams(vmem_limit_bytes=32 << 20),
        name="correlate",
        cost_estimate=pl.CostEstimate(
            flops=4 * BLOCK * SPAN * LAGS * TOTAL, bytes_accessed=8 << 20, transcendentals=0
        ),
    )(core, column, *straight, *crossed)


def up(value, steps):
    pairs = [(source, (source - steps) % ROWS) for source in range(ROWS)]
    return lax.ppermute(value, "row", pairs)


def body(samples, taps):
    core = lax.axis_index("core")
    parts = filter_bank(samples, taps[None], cosine_matrix())
    parts = lax.all_to_all(parts, ("sub", "core"), split_axis=0, concat_axis=0, tiled=True)
    mine = assemble(parts)
    above, second = up(mine, 1), up(mine, 2)
    beside = lax.ppermute(mine, "column", [(0, 1), (1, 0)])
    held = [
        mine,
        above,
        second,
        beside,
        up(beside, 1),
        lax.ppermute(second, "column", [(0, 1)]),
    ]
    swapped = [lax.ppermute(value, "core", [(0, 1), (1, 0)]) for value in held]
    held[0] = lax.ppermute(swapped[0], "core", [(0, 1), (1, 0)])
    column = lax.axis_index("column")
    return correlate(core[None], column[None], held, swapped)


def solution(mesh):
    inner = Mesh(mesh.devices.reshape(N_SUB, ROWS, 2, 2), ("sub", "row", "column", "core"))
    stations = ("row", "column", "core")
    in_specs = (P(stations, "sub"), P())
    out_specs = P("sub", stations, None, None)
    return jax.shard_map(body, mesh=inner, in_specs=in_specs, out_specs=out_specs, check_vma=False)
```

```python
import functools
import math

import jax
import jax.numpy as jnp
import numpy as np
from jax import lax
from jax.experimental import pallas as pl
from jax.experimental.pallas import tpu as pltpu
from jax.sharding import Mesh
from jax.sharding import PartitionSpec as P

BRANCHES = 256
TAPS = 16
LAGS = 128
T_DEV = 256
SUBBANDS = 16
BLOCK = 32
N_SUB = 8
ROWS = 4
TOTAL = T_DEV * N_SUB
TAIL = 128
CHUNK = 32
REACH = 4
LANE = 128
PITCH = 40


def cosine_matrix():
    band = np.float32(BRANCHES // 2 - SUBBANDS // 2) + np.arange(SUBBANDS, dtype=np.float32)
    band = band + np.float32(0.5)
    arm = np.arange(BRANCHES, dtype=np.float32) + np.float32(0.5)
    angle = np.float32(math.pi / BRANCHES) * band[:, None] * arm[None, :]
    table = np.cos(angle) * np.float32(math.sqrt(2.0 / BRANCHES) / 512.0)
    return jnp.asarray(table).astype(jnp.bfloat16).astype(jnp.float32)


def nt_dot(a, b):
    return lax.dot_general(a, b, (((1,), (1,)), ((), ())), preferred_element_type=jnp.float32)


def shift_lanes(tiles, steps, lane, grow):
    rolled = [pltpu.roll(t, steps, 1) for t in tiles]
    outside = jnp.zeros_like(rolled[0])
    result = [jnp.where(lane < steps, outside, rolled[0])]
    for before, after in zip(rolled[:-1], rolled[1:]):
        result.append(jnp.where(lane < steps, before, after))
    if grow:
        result.append(jnp.where(lane < steps, rolled[-1], outside))
    return result


def filter_kernel(
    x_hbm, taps_hbm, cos_hbm, out_ref, x_ref, taps_ref, cos_ref, frames_ref, weight_ref, bands_ref, sems
):
    def fetch(c):
        columns = pl.ds(c * CHUNK * BRANCHES, CHUNK * BRANCHES)
        return pltpu.make_async_copy(x_hbm.at[:, columns], x_ref.at[:, columns], sems.at[c])

    chunks = T_DEV // CHUNK
    taps_copy = pltpu.make_async_copy(taps_hbm, taps_ref, sems.at[chunks])
    cos_copy = pltpu.make_async_copy(cos_hbm, cos_ref, sems.at[chunks + 1])
    taps_copy.start()
    cos_copy.start()
    for c in range(chunks):
        fetch(c).start()
    taps_copy.wait()
    cos_copy.wait()
    table = cos_ref[...]
    for tap in range(TAPS):
        coefficients = taps_ref[:, tap * BRANCHES : (tap + 1) * BRANCHES].astype(jnp.float32)
        product = table * coefficients
        high = product.astype(jnp.bfloat16)
        low = (product - high.astype(jnp.float32)).astype(jnp.bfloat16)
        weight_ref[0, tap * SUBBANDS : (tap + 1) * SUBBANDS, :] = high
        weight_ref[1, tap * SUBBANDS : (tap + 1) * SUBBANDS, :] = low

    for c in range(chunks):
        fetch(c).wait()

        def one_frame(frame, carry):
            row = pl.multiple_of(frame * PITCH, 8)
            for half in range(2):
                start = pl.multiple_of(frame * BRANCHES + half * LANE, LANE)
                frames_ref[half, pl.ds(row, BLOCK), :] = x_ref[:, pl.ds(start, LANE)].astype(
                    jnp.float32
                )
            return carry

        lax.fori_loop(c * CHUNK, (c + 1) * CHUNK, one_frame, 0, unroll=8)

    lane = lax.broadcasted_iota(jnp.int32, (SUBBANDS, LANE), 1)

    def one_input(i, carry):
        data = jnp.concatenate(
            [frames_ref[half, pl.ds(i, T_DEV, stride=PITCH), :] for half in range(2)], axis=1
        ).astype(jnp.bfloat16)
        products = nt_dot(weight_ref[0], data) + nt_dot(weight_ref[1], data)
        level = []
        for tap in range(TAPS):
            part = products[tap * SUBBANDS : (tap + 1) * SUBBANDS]
            level.append([part[:, :LANE], part[:, LANE:]])
        steps = 1
        while len(level) > 1:
            merged = []
            for first, second in zip(level[0::2], level[1::2]):
                moved = shift_lanes(first, steps, lane, grow=len(first) == 2)
                total = [m + s for m, s in zip(moved, second)]
                merged.append(total + moved[len(second) :])
            level = merged
            steps *= 2
        for tile, value in enumerate(level[0]):
            bands_ref[tile, pl.ds(i, SUBBANDS, stride=PITCH), :] = value
        return carry

    lax.fori_loop(0, BLOCK, one_input, 0, unroll=16)
    for tile in range(3):
        out_ref[:, :, tile * LANE : (tile + 1) * LANE] = (
            bands_ref[tile].reshape(SUBBANDS, PITCH, LANE)[:, :BLOCK].astype(jnp.bfloat16)
        )


def filter_bank(samples, taps, table):
    return pl.pallas_call(
        filter_kernel,
        in_specs=[pl.BlockSpec(memory_space=pl.ANY)] * 3,
        out_specs=pl.BlockSpec(memory_space=pltpu.VMEM),
        out_shape=jax.ShapeDtypeStruct((SUBBANDS, BLOCK, T_DEV + TAIL), jnp.bfloat16),
        scratch_shapes=[
            pltpu.VMEM((BLOCK, T_DEV * BRANCHES), jnp.bfloat16),
            pltpu.VMEM((1, TAPS * BRANCHES), jnp.int32),
            pltpu.VMEM((SUBBANDS, BRANCHES), jnp.float32),
            pltpu.VMEM((2, T_DEV * PITCH, LANE), jnp.float32),
            pltpu.VMEM((2, TAPS * SUBBANDS, BRANCHES), jnp.bfloat16),
            pltpu.VMEM((3, SUBBANDS * PITCH, LANE), jnp.float32),
            pltpu.SemaphoreType.DMA((T_DEV // CHUNK + 2,)),
        ],
        compiler_params=pltpu.CompilerParams(vmem_limit_bytes=60 << 20),
        name="filter_bank",
    )(samples, taps, table)


def assemble_kernel(parts_ref, out_ref):
    for band in range(2):
        rows = slice(band * BLOCK, (band + 1) * BLOCK)
        for block in range(N_SUB):
            here = parts_ref[block * 2 + band]
            start = block * T_DEV
            head = here[:, :LANE]
            if block:
                tail = parts_ref[(block - 1) * 2 + band][:, T_DEV:]
                head = (head.astype(jnp.float32) + tail.astype(jnp.float32)).astype(jnp.bfloat16)
            out_ref[rows, start : start + LANE] = head
            out_ref[rows, start + LANE : start + T_DEV] = here[:, LANE:T_DEV]


def assemble(parts):
    return pl.pallas_call(
        assemble_kernel,
        out_shape=jax.ShapeDtypeStruct((2 * BLOCK, TOTAL), jnp.bfloat16),
        name="assemble",
    )(parts)


PAIRS = 8
SPAN = 9 * BLOCK


def build_rows(own_ref, target_ref, slot, first, mask):
    for a in range(2):
        before = None
        for tile in range(TOTAL // LANE + 1):
            row = own_ref[tile, pl.ds(first + a, 1), :]
            rolled = pltpu.roll(
                jnp.broadcast_to(row, (LAGS, LANE)), 0, 1, stride=1, stride_axis=0
            )
            if tile:
                target_ref[slot, a * LAGS : (a + 1) * LAGS, (tile - 1) * LANE : tile * LANE] = (
                    jnp.where(mask, rolled, before).astype(jnp.bfloat16)
                )
            before = rolled


HELD = 6


def chip_source(j, column):
    return {0: (0, 0), 1: (3, 4), 2: (1, 1), 3: (4, 5), 4: (2, 2)}[j][column]


def correlate_kernel(core_ref, column_ref, *refs):
    count = HELD
    straight, crossed = refs[:count], refs[count : 2 * count]
    out_ref, own_ref, span_ref, rows_ref = refs[2 * count :]
    band = pl.program_id(0)
    step = pl.program_id(1)
    row = lax.broadcasted_iota(jnp.int32, (LAGS, LANE), 0)
    mask = lax.broadcasted_iota(jnp.int32, (LAGS, LANE), 1) >= row
    core = core_ref[0]
    column = column_ref[0]

    def gather(s):
        part = slice(s * BLOCK, (s + 1) * BLOCK)
        for k in range(SPAN // BLOCK):
            place = slice(k * BLOCK, (k + 1) * BLOCK)
            arrays = crossed if k % 2 else straight
            cases = {}
            for number in range(2):
                for half in range(2):
                    j = (half + k) // 2
                    cases.setdefault(chip_source(j, number), []).append((number, half))
            for source, which in cases.items():
                if len(which) == 4:
                    span_ref[place, :] = arrays[source][part, :]
                    continue
                here = functools.reduce(
                    jnp.logical_or, [(column == number) & (core == half) for number, half in which]
                )

                @pl.when(here)
                def _():
                    span_ref[place, :] = arrays[source][part, :]

        own = span_ref[:BLOCK, :].astype(jnp.float32)
        half = jnp.zeros((BLOCK, LAGS // 2), jnp.float32)
        padded = jnp.concatenate([half, own, half], axis=1)
        for tile in range(TOTAL // LANE + 1):
            own_ref[tile] = padded[:, tile * LANE : (tile + 1) * LANE]
        build_rows(own_ref, rows_ref, 0, 0, mask)

    @pl.when(jnp.logical_and(step == 0, band == 0))
    def _():
        gather(0)

    @pl.when(jnp.logical_and(step == 0, band == 1))
    def _():
        gather(1)

    scale = 1.0 / math.sqrt(TOTAL)
    for pair in range(PAIRS):
        index = step * PAIRS + pair
        result = nt_dot(span_ref[...], rows_ref[pair % 2]) * scale
        following = jnp.minimum(index + 1, BLOCK // 2 - 1)
        build_rows(own_ref, rows_ref, (pair + 1) % 2, 2 * following, mask)
        out_ref[0, 2 * pair] = result[:, :LAGS].astype(jnp.bfloat16)
        out_ref[0, 2 * pair + 1] = result[:, LAGS:].astype(jnp.bfloat16)


def correlate(core, column, straight, crossed):
    steps = BLOCK // (2 * PAIRS)
    held = pl.BlockSpec(memory_space=pltpu.VMEM)
    return pl.pallas_call(
        correlate_kernel,
        grid_spec=pltpu.PrefetchScalarGridSpec(
            num_scalar_prefetch=2,
            grid=(2, steps),
            in_specs=[held] * (2 * HELD),
            out_specs=pl.BlockSpec(
                (1, 2 * PAIRS, SPAN, LAGS), lambda s, c, w, v: (s, c, 0, 0)
            ),
            scratch_shapes=[
                pltpu.VMEM((TOTAL // LANE + 1, BLOCK, LANE), jnp.float32),
                pltpu.VMEM((SPAN, TOTAL), jnp.bfloat16),
                pltpu.VMEM((2, 2 * LAGS, TOTAL), jnp.bfloat16),
            ],
        ),
        out_shape=jax.ShapeDtypeStruct((2, BLOCK, SPAN, LAGS), jnp.bfloat16),
        compiler_params=pltpu.CompilerParams(vmem_limit_bytes=32 << 20),
        name="correlate",
        cost_estimate=pl.CostEstimate(
            flops=4 * BLOCK * SPAN * LAGS * TOTAL, bytes_accessed=8 << 20, transcendentals=0
        ),
    )(core, column, *straight, *crossed)


def up(value, steps):
    pairs = [(source, (source - steps) % ROWS) for source in range(ROWS)]
    return lax.ppermute(value, "row", pairs)


def body(samples, taps):
    core = lax.axis_index("core")
    parts = filter_bank(samples, taps[None], cosine_matrix())
    parts = lax.all_to_all(parts, "sub", split_axis=0, concat_axis=0, tiled=True)
    mine = assemble(parts)
    above, second = up(mine, 1), up(mine, 2)
    beside = lax.ppermute(mine, "column", [(0, 1), (1, 0)])
    held = [
        mine,
        above,
        second,
        beside,
        up(beside, 1),
        lax.ppermute(second, "column", [(0, 1)]),
    ]
    swapped = [lax.ppermute(value, "core", [(0, 1), (1, 0)]) for value in held]
    held[0] = lax.ppermute(swapped[0], "core", [(0, 1), (1, 0)])
    column = lax.axis_index("column")
    return correlate(core[None], column[None], held, swapped)


def solution(mesh):
    inner = Mesh(mesh.devices.reshape(N_SUB, ROWS, 2, 2), ("sub", "row", "column", "core"))
    stations = ("row", "column", "core")
    in_specs = (P(stations, "sub"), P())
    out_specs = P("sub", stations, None, None)
    return jax.shard_map(body, mesh=inner, in_specs=in_specs, out_specs=out_specs, check_vma=False)
```

```python
import functools
import math

import jax
import jax.numpy as jnp
import numpy as np
from jax import lax
from jax.experimental import pallas as pl
from jax.experimental.pallas import tpu as pltpu
from jax.sharding import Mesh
from jax.sharding import PartitionSpec as P

BRANCHES = 256
TAPS = 16
LAGS = 128
T_DEV = 256
SUBBANDS = 16
BLOCK = 32
N_SUB = 8
ROWS = 4
TOTAL = T_DEV * N_SUB
TAIL = 128
CHUNK = 32
REACH = 4
LANE = 128
PITCH = 40


def cosine_matrix():
    band = np.float32(BRANCHES // 2 - SUBBANDS // 2) + np.arange(SUBBANDS, dtype=np.float32)
    band = band + np.float32(0.5)
    arm = np.arange(BRANCHES, dtype=np.float32) + np.float32(0.5)
    angle = np.float32(math.pi / BRANCHES) * band[:, None] * arm[None, :]
    table = np.cos(angle) * np.float32(math.sqrt(2.0 / BRANCHES) / 512.0)
    return jnp.asarray(table).astype(jnp.bfloat16).astype(jnp.float32)


def nt_dot(a, b):
    return lax.dot_general(a, b, (((1,), (1,)), ((), ())), preferred_element_type=jnp.float32)


def shift_lanes(tiles, steps, lane, grow):
    rolled = [pltpu.roll(t, steps, 1) for t in tiles]
    outside = jnp.zeros_like(rolled[0])
    result = [jnp.where(lane < steps, outside, rolled[0])]
    for before, after in zip(rolled[:-1], rolled[1:]):
        result.append(jnp.where(lane < steps, before, after))
    if grow:
        result.append(jnp.where(lane < steps, rolled[-1], outside))
    return result


def filter_kernel(
    x_hbm, taps_hbm, cos_hbm, out_ref, x_ref, taps_ref, cos_ref, frames_ref, weight_ref, bands_ref, sems
):
    def fetch(c):
        columns = pl.ds(c * CHUNK * BRANCHES, CHUNK * BRANCHES)
        return pltpu.make_async_copy(x_hbm.at[:, columns], x_ref.at[:, columns], sems.at[c])

    chunks = T_DEV // CHUNK
    taps_copy = pltpu.make_async_copy(taps_hbm, taps_ref, sems.at[chunks])
    cos_copy = pltpu.make_async_copy(cos_hbm, cos_ref, sems.at[chunks + 1])
    taps_copy.start()
    cos_copy.start()
    for c in range(chunks):
        fetch(c).start()
    taps_copy.wait()
    cos_copy.wait()
    table = cos_ref[...]
    for tap in range(TAPS):
        coefficients = taps_ref[:, tap * BRANCHES : (tap + 1) * BRANCHES].astype(jnp.float32)
        product = table * coefficients
        high = product.astype(jnp.bfloat16)
        low = (product - high.astype(jnp.float32)).astype(jnp.bfloat16)
        weight_ref[0, tap * SUBBANDS : (tap + 1) * SUBBANDS, :] = high
        weight_ref[1, tap * SUBBANDS : (tap + 1) * SUBBANDS, :] = low

    for c in range(chunks):
        fetch(c).wait()

        def one_frame(frame, carry):
            row = pl.multiple_of(frame * PITCH, 8)
            for half in range(2):
                start = pl.multiple_of(frame * BRANCHES + half * LANE, LANE)
                frames_ref[half, pl.ds(row, BLOCK), :] = x_ref[:, pl.ds(start, LANE)].astype(
                    jnp.float32
                )
            return carry

        lax.fori_loop(c * CHUNK, (c + 1) * CHUNK, one_frame, 0, unroll=8)

    lane = lax.broadcasted_iota(jnp.int32, (SUBBANDS, LANE), 1)

    def one_input(i, carry):
        data = jnp.concatenate(
            [frames_ref[half, pl.ds(i, T_DEV, stride=PITCH), :] for half in range(2)], axis=1
        ).astype(jnp.bfloat16)
        products = nt_dot(weight_ref[0], data) + nt_dot(weight_ref[1], data)
        level = []
        for tap in range(TAPS):
            part = products[tap * SUBBANDS : (tap + 1) * SUBBANDS]
            level.append([part[:, :LANE], part[:, LANE:]])
        steps = 1
        while len(level) > 1:
            merged = []
            for first, second in zip(level[0::2], level[1::2]):
                moved = shift_lanes(first, steps, lane, grow=len(first) == 2)
                total = [m + s for m, s in zip(moved, second)]
                merged.append(total + moved[len(second) :])
            level = merged
            steps *= 2
        for tile, value in enumerate(level[0]):
            bands_ref[tile, pl.ds(i, SUBBANDS, stride=PITCH), :] = value
        return carry

    lax.fori_loop(0, BLOCK, one_input, 0, unroll=16)
    for tile in range(3):
        out_ref[:, :, tile * LANE : (tile + 1) * LANE] = (
            bands_ref[tile].reshape(SUBBANDS, PITCH, LANE)[:, :BLOCK].astype(jnp.bfloat16)
        )


def filter_bank(samples, taps, table):
    return pl.pallas_call(
        filter_kernel,
        in_specs=[pl.BlockSpec(memory_space=pl.ANY)] * 3,
        out_specs=pl.BlockSpec(memory_space=pltpu.VMEM),
        out_shape=jax.ShapeDtypeStruct((SUBBANDS, BLOCK, T_DEV + TAIL), jnp.bfloat16),
        scratch_shapes=[
            pltpu.VMEM((BLOCK, T_DEV * BRANCHES), jnp.bfloat16),
            pltpu.VMEM((1, TAPS * BRANCHES), jnp.int32),
            pltpu.VMEM((SUBBANDS, BRANCHES), jnp.float32),
            pltpu.VMEM((2, T_DEV * PITCH, LANE), jnp.float32),
            pltpu.VMEM((2, TAPS * SUBBANDS, BRANCHES), jnp.bfloat16),
            pltpu.VMEM((3, SUBBANDS * PITCH, LANE), jnp.float32),
            pltpu.SemaphoreType.DMA((T_DEV // CHUNK + 2,)),
        ],
        compiler_params=pltpu.CompilerParams(vmem_limit_bytes=60 << 20),
        name="filter_bank",
    )(samples, taps, table)


def assemble_kernel(parts_ref, out_ref):
    for band in range(2):
        rows = slice(band * BLOCK, (band + 1) * BLOCK)
        for block in range(N_SUB):
            here = parts_ref[block * 2 + band]
            start = block * T_DEV
            head = here[:, :LANE]
            if block:
                tail = parts_ref[(block - 1) * 2 + band][:, T_DEV:]
                head = (head.astype(jnp.float32) + tail.astype(jnp.float32)).astype(jnp.bfloat16)
            out_ref[rows, start : start + LANE] = head
            out_ref[rows, start + LANE : start + T_DEV] = here[:, LANE:T_DEV]


def assemble(parts):
    return pl.pallas_call(
        assemble_kernel,
        out_shape=jax.ShapeDtypeStruct((2 * BLOCK, TOTAL), jnp.bfloat16),
        name="assemble",
    )(parts)


PAIRS = 8
SPAN = 9 * BLOCK


def build_rows(own_ref, target_ref, slot, first, mask):
    for a in range(2):
        before = None
        for tile in range(TOTAL // LANE + 1):
            row = own_ref[tile, pl.ds(first + a, 1), :]
            rolled = pltpu.roll(
                jnp.broadcast_to(row, (LAGS, LANE)), 0, 1, stride=1, stride_axis=0
            )
            if tile:
                target_ref[slot, a * LAGS : (a + 1) * LAGS, (tile - 1) * LANE : tile * LANE] = (
                    jnp.where(mask, rolled, before).astype(jnp.bfloat16)
                )
            before = rolled


HELD = 6


def chip_source(j, column):
    return {0: (0, 0), 1: (3, 4), 2: (1, 1), 3: (4, 5), 4: (2, 2)}[j][column]


def correlate_kernel(core_ref, column_ref, *refs):
    count = HELD
    straight, crossed = refs[:count], refs[count : 2 * count]
    out_ref, own_ref, span_ref, rows_ref = refs[2 * count :]
    band = pl.program_id(0)
    step = pl.program_id(1)
    row = lax.broadcasted_iota(jnp.int32, (LAGS, LANE), 0)
    mask = lax.broadcasted_iota(jnp.int32, (LAGS, LANE), 1) >= row
    core = core_ref[0]
    column = column_ref[0]

    def gather(s):
        part = slice(s * BLOCK, (s + 1) * BLOCK)
        for k in range(SPAN // BLOCK):
            place = slice(k * BLOCK, (k + 1) * BLOCK)
            arrays = crossed if k % 2 else straight
            cases = {}
            for number in range(2):
                for half in range(2):
                    j = (half + k) // 2
                    cases.setdefault(chip_source(j, number), []).append((number, half))
            for source, which in cases.items():
                if len(which) == 4:
                    span_ref[place, :] = arrays[source][part, :]
                    continue
                here = functools.reduce(
                    jnp.logical_or, [(column == number) & (core == half) for number, half in which]
                )

                @pl.when(here)
                def _():
                    span_ref[place, :] = arrays[source][part, :]

        own = span_ref[:BLOCK, :].astype(jnp.float32)
        half = jnp.zeros((BLOCK, LAGS // 2), jnp.float32)
        padded = jnp.concatenate([half, own, half], axis=1)
        for tile in range(TOTAL // LANE + 1):
            own_ref[tile] = padded[:, tile * LANE : (tile + 1) * LANE]
        build_rows(own_ref, rows_ref, 0, 0, mask)

    @pl.when(jnp.logical_and(step == 0, band == 0))
    def _():
        gather(0)

    @pl.when(jnp.logical_and(step == 0, band == 1))
    def _():
        gather(1)

    scale = 1.0 / math.sqrt(TOTAL)
    for pair in range(PAIRS):
        index = step * PAIRS + pair
        result = nt_dot(span_ref[...], rows_ref[pair % 2]) * scale
        following = jnp.minimum(index + 1, BLOCK // 2 - 1)
        build_rows(own_ref, rows_ref, (pair + 1) % 2, 2 * following, mask)
        out_ref[0, 2 * pair] = result[:, :LAGS].astype(jnp.bfloat16)
        out_ref[0, 2 * pair + 1] = result[:, LAGS:].astype(jnp.bfloat16)


def correlate(core, column, straight, crossed):
    steps = BLOCK // (2 * PAIRS)
    held = pl.BlockSpec(memory_space=pltpu.VMEM)
    return pl.pallas_call(
        correlate_kernel,
        grid_spec=pltpu.PrefetchScalarGridSpec(
            num_scalar_prefetch=2,
            grid=(2, steps),
            in_specs=[held] * (2 * HELD),
            out_specs=pl.BlockSpec(
                (1, 2 * PAIRS, SPAN, LAGS), lambda s, c, w, v: (s, c, 0, 0)
            ),
            scratch_shapes=[
                pltpu.VMEM((TOTAL // LANE + 1, BLOCK, LANE), jnp.float32),
                pltpu.VMEM((SPAN, TOTAL), jnp.bfloat16),
                pltpu.VMEM((2, 2 * LAGS, TOTAL), jnp.bfloat16),
            ],
        ),
        out_shape=jax.ShapeDtypeStruct((2, BLOCK, SPAN, LAGS), jnp.bfloat16),
        compiler_params=pltpu.CompilerParams(vmem_limit_bytes=32 << 20),
        name="correlate",
        cost_estimate=pl.CostEstimate(
            flops=4 * BLOCK * SPAN * LAGS * TOTAL, bytes_accessed=8 << 20, transcendentals=0
        ),
    )(core, column, *straight, *crossed)


def up(value, steps):
    pairs = [(source, (source - steps) % ROWS) for source in range(ROWS)]
    return lax.ppermute(value, "row", pairs)


def body(samples, taps):
    core = lax.axis_index("core")
    parts = filter_bank(samples, taps[None], cosine_matrix())
    parts = lax.all_to_all(parts, "sub", split_axis=0, concat_axis=0, tiled=True)
    mine = assemble(parts)
    above, second = up(mine, 1), up(mine, 2)
    beside = lax.ppermute(mine, "column", [(0, 1), (1, 0)])
    held = [
        mine,
        above,
        second,
        beside,
        up(beside, 1),
        lax.ppermute(second, "column", [(0, 1)]),
    ]
    swapped = [lax.ppermute(value, "core", [(0, 1), (1, 0)]) for value in held]
    held[0] = lax.ppermute(swapped[0], "core", [(0, 1), (1, 0)])
    swapped[2] = lax.ppermute(second, "core", [(0, 1)])
    column = lax.axis_index("column")
    return correlate(core[None], column[None], held, swapped)


def solution(mesh):
    inner = Mesh(mesh.devices.reshape(N_SUB, ROWS, 2, 2), ("sub", "row", "column", "core"))
    stations = ("row", "column", "core")
    in_specs = (P(stations, "sub"), P())
    out_specs = P("sub", stations, None, None)
    return jax.shard_map(body, mesh=inner, in_specs=in_specs, out_specs=out_specs, check_vma=False)
```
